32 devices in a mesh: tile: 8 (over z, x), lev: 4 (over y, core).
Axes of the slice: x: 2, y: 2, z: 4, core: 2. Of those that a mesh axis runs over, the one named last changes fastest.
Arguments:
- theta: float32 [128, 32, 1024], P('lev', None, 'tile'), may hold values from -6 to 6
- thickness: float32 [128, 32, 1024], P('lev', None, 'tile'), may hold values from 0.5 to 1.5
- wind: float32 [128, 32, 1024], P('lev', None, 'tile'), may hold values from -6 to 6
- surface: float32 [32, 1024], P(None, 'tile'), may hold values from -6 to 6
- trigger: int32 [32, 1024], P(None, 'tile'), may hold values 0 or 1
- closure: int32 [32, 1024], P(None, 'tile'), may hold values from 0 to 2
- closure_weights: bfloat16 [4, 128, 128], replicated, may hold values from -0.5 to 0.5
Outputs:
- pressure: float32 [128, 32, 1024], P('lev', None, 'tile')
- wind_next: float32 [128, 32, 1024], P('lev', None, 'tile')
- heating: bfloat16 [128, 32, 1024], P('lev', None, 'tile')
The draws below stay inside these ranges and needn't reach their ends.
Inputs may be any that keep to these rules, and one draw needn't show every extreme that they name: trigger[r, c] is 0 or 1 in every draw. closure[r, c] is one of 0 .. 2 in every draw.
All inputs are finite; a program needn't handle non-finite values. No bound on the sum of `trigger` on one device may be relied on, other than what follows from the above.
Results may differ from the reference program's by a relative error of at most 0.0049.
Values may be sent and summed in bfloat16 or wider, within the bound.
A program may use at most 64 MiB of HBM per device.

```python
import jax
import jax.numpy as jnp
from jax import lax

LEVELS = 128
CLOSURES = 3
SUBSTEPS = 6
ROWS = 32
LONS = 1024


def with_ends(array, rng, smallest, top_value):
    index_at = [jax.random.randint(jax.random.fold_in(rng, axis), (), 0, length) for axis, length in enumerate(array.shape)]
    widest = array.shape.index(max(array.shape))
    neighbour = index_at[:widest] + [(index_at[widest] + 1) % array.shape[widest]] + index_at[widest + 1:]
    return array.at[tuple(index_at)].set(smallest).at[tuple(neighbour)].set(top_value)


def block_levels(key, dims, split, least, largest):
    gain, own = 1.0, jax.random.fold_in(key, 6)
    for position, shards_of in split:
        draws = jnp.exp(jax.random.uniform(jax.random.fold_in(own, position), (shards_of,), jnp.float32, least / len(split), largest / len(split)))
        gain = gain * jnp.repeat(draws, dims[position] // shards_of).reshape([-1 if axis == position else 1 for axis in range(len(dims))])
    return gain


def centred(rng, shape, spread, bound, split=(), dtype=jnp.bfloat16):
    entries = spread * jax.random.normal(rng, shape, jnp.float32)
    if split:
        entries = entries * block_levels(rng, shape, split, -0.22, 0.18)
    return jnp.clip(entries, -bound, bound).astype(dtype)


def setup_inputs(seed: int = 0) -> dict:
    streams_of = jax.random.split(jax.random.key(seed), 8)
    theta = centred(streams_of[0], (LEVELS, ROWS, LONS), 1.0, 6.0, ((0, 4), (2, 8)), jnp.float32)
    thickness = jnp.clip(0.5 + 1.0 * jax.random.uniform(streams_of[1], (LEVELS, ROWS, LONS), jnp.float32) ** block_levels(streams_of[1], (LEVELS, ROWS, LONS), ((0, 4), (2, 8)), -0.2, 0.2), 0.5, 1.5)
    wind = centred(streams_of[2], (LEVELS, ROWS, LONS), 1.0, 6.0, ((0, 4), (2, 8)), jnp.float32)
    surface = centred(streams_of[3], (ROWS, LONS), 1.0, 6.0, ((1, 8),), jnp.float32)
    trigger = with_ends((jax.random.randint(streams_of[4], (ROWS, LONS), 0, 2) < 1).astype(jnp.int32), jax.random.fold_in(streams_of[4], 1), 0, 1)
    closure = with_ends(jax.random.randint(streams_of[5], (ROWS, LONS), 0, CLOSURES), jax.random.fold_in(streams_of[5], 1), 0, CLOSURES - 1).astype(jnp.int32)
    closure_weights = centred(streams_of[6], (CLOSURES + 1, LEVELS, LEVELS), LEVELS ** -0.5, 0.5)
    return dict(theta=theta, thickness=thickness, wind=wind, surface=surface, trigger=trigger, closure=closure, closure_weights=closure_weights)


courant = 0.9


def reference(theta, thickness, wind, surface, trigger, closure, closure_weights):
    thermal = theta * thickness * (LEVELS ** -0.5)
    suffix = lax.cumsum(thermal, axis=0, reverse=True) - thermal
    geopot = surface[None, :, :] + suffix + 0.5 * thermal
    pressure = geopot
    velocity = wind
    for substep in range(SUBSTEPS):
        velocity = velocity - courant * (jnp.roll(pressure, -1, axis=2) - pressure)
        pressure = pressure - courant * (velocity - jnp.roll(velocity, 1, axis=2))
    column = theta.astype(jnp.bfloat16).reshape((LEVELS, ROWS * LONS))
    boundary = jnp.dot(closure_weights[CLOSURES], column, preferred_element_type=jnp.float32).reshape((LEVELS, ROWS, LONS))
    convect = jnp.zeros(theta.shape, jnp.float32)
    for scheme in range(CLOSURES):
        answer = jnp.dot(closure_weights[scheme], column, preferred_element_type=jnp.float32).reshape((LEVELS, ROWS, LONS))
        convect = convect + jnp.where(closure[None, :, :] == scheme, answer, jnp.float32(0.0))
    heating = (boundary + trigger.astype(jnp.float32)[None, :, :] * convect).astype(jnp.bfloat16)
    return pressure, velocity, heating
```

```python
import functools

import jax
import jax.numpy as jnp
import ml_dtypes
import numpy as np
from jax import lax
from jax.experimental import pallas as pl
from jax.experimental.pallas import tpu as pltpu
from jax.sharding import PartitionSpec as P

LEVELS = 128
SUBSTEPS = 6
SLOT = 16
CHUNK = 8
PACK = 16

courant = 0.9
F32 = jnp.float32
BF16 = jnp.bfloat16
MESH = pl.DeviceIdType.MESH


def substep_operator(width):
    halo = SUBSTEPS
    pad = 2 * halo
    pressure = np.zeros((2 * width, width + 2 * pad))
    velocity = np.zeros_like(pressure)
    cells = np.arange(width)
    pressure[cells, pad + cells] = 1.0
    velocity[width + cells, pad + cells] = 1.0
    for substep in range(SUBSTEPS):
        velocity = velocity - courant * (np.roll(pressure, -1, axis=1) - pressure)
        pressure = pressure - courant * (velocity - np.roll(velocity, 1, axis=1))
    spare = np.zeros((2 * width, width - 2 * halo))
    before, after = slice(pad - halo, pad), slice(pad + width, pad + width + halo)
    inside = slice(pad, pad + width)
    whole = np.concatenate(
        [
            pressure[:, inside], velocity[:, inside],
            pressure[:, before], velocity[:, before], spare,
            pressure[:, after], velocity[:, after], spare,
        ],
        axis=1,
    ).astype(np.float32)
    high = whole.astype(ml_dtypes.bfloat16)
    low = (whole - high.astype(np.float32)).astype(ml_dtypes.bfloat16)
    return high, low


def split(value):
    high = value.astype(BF16)
    return high, (value - high.astype(F32)).astype(BF16)


def dot(a, b):
    return jnp.dot(a, b, preferred_element_type=F32)


def kernel(
    dims,
    theta, thick, wind, surf, trig, clos, wts, mhi, mlo,
    p_out, v_out, h_out,
    theta_v, thick_v, wind_v, surf_v, trig_v, clos_v, w_v, mhi_v, mlo_v,
    gath, xh, xl, p_s, v_s, pack, pack_in, tot, tot_in, cpack, cpack_in, heat, hout,
    in_sem, out_sem, hout_sem, dir_send, dir_recv, par_send, par_recv,
    tot_send, tot_recv, halo_send, halo_recv, chalo_send, chalo_recv,
):
    levs, tiles, L, R, C, S = dims
    half = levs // 2
    chunks = R // CHUNK
    slots = C // SLOT
    srows = L * R // slots
    H = SUBSTEPS
    me = lax.axis_index("lev")
    here = lax.axis_index("tile")
    mate = me + 1 - 2 * (me % 2)
    right, left = (here + 1) % tiles, (here + tiles - 1) % tiles

    loads = [
        pltpu.make_async_copy(src, dst, in_sem.at[i])
        for i, (src, dst) in enumerate(
            [
                (theta, theta_v), (thick, thick_v), (surf, surf_v), (wind, wind_v), (mhi, mhi_v), (mlo, mlo_v),
                (wts.at[:, pl.ds(pl.multiple_of(me * L, 16), L), :], w_v), (trig, trig_v), (clos, clos_v),
            ]
        )
    ]
    for copy in loads:
        copy.start()
    barrier = pltpu.get_barrier_semaphore()
    for d in range(1, levs):
        pl.semaphore_signal(barrier, inc=1, device_id=(here, (me + d) % levs), device_id_type=MESH)
    for side in (left, right):
        pl.semaphore_signal(barrier, inc=1, device_id=(side, me), device_id_type=MESH)

    def slot_of(rank):
        return pl.ds(pl.multiple_of(rank * L, 16), L)

    def block_copy(owner, c, send, recv, target):
        block = gath.at[pl.ds(c * CHUNK, CHUNK), slot_of(owner), :]
        return pltpu.make_async_remote_copy(
            src_ref=block, dst_ref=block, send_sem=send, recv_sem=recv, device_id=(here, target), device_id_type=MESH
        )

    def direct(d, c):
        return block_copy(me, c, dir_send.at[d - 1, c], dir_recv.at[d - 1, c], (me + 2 * d) % levs)

    def to_mate(d, c):
        return block_copy((me + levs - 2 * d) % levs, c, par_send.at[d, c], par_recv.at[d, c], mate)

    def direct_in(d, c):
        return block_copy(
            (me + levs - 2 * d) % levs, c, dir_send.at[d - 1, c], dir_recv.at[d - 1, c], (me + 2 * d) % levs
        )

    def from_mate(d, c):
        return block_copy((mate + levs - 2 * d) % levs, c, par_send.at[d, c], par_recv.at[d, c], mate)

    loads[0].wait()
    for c in range(chunks):
        def relayout(i, _, c=c):
            r = c * CHUNK + i
            gath[r, slot_of(me), :] = theta_v[pl.ds(r, L, stride=R), :].astype(BF16)
            return 0

        lax.fori_loop(0, CHUNK, relayout, 0, unroll=True)
        if c == 0:
            pl.semaphore_wait(barrier, levs + 1)
        for d in range(1, half):
            direct(d, c).start()
        to_mate(0, c).start()

    for i in (1, 2, 3):
        loads[i].wait()

    def level(i, total):
        rows = pl.ds(pl.multiple_of((L - 1 - i) * R, R), R)
        thermal = theta_v[rows, :] * thick_v[rows, :] * LEVELS ** (-0.5)
        geopot = surf_v[...] + total + 0.5 * thermal
        xh[rows, 0:C], xl[rows, 0:C] = split(geopot)
        xh[rows, C : 2 * C], xl[rows, C : 2 * C] = split(wind_v[rows, :])
        return total + thermal

    tot[...] = lax.fori_loop(0, L, level, jnp.zeros((R, C), F32), unroll=4)

    def total_copy(d):
        return pltpu.make_async_remote_copy(
            src_ref=tot, dst_ref=tot_in.at[d - 1], send_sem=tot_send.at[d - 1], recv_sem=tot_recv.at[d - 1],
            device_id=(here, (me + d) % levs), device_id_type=MESH,
        )

    for d in range(1, levs):
        total_copy(d).start()

    loads[4].wait()
    loads[5].wait()
    per = 2
    for step in range(slots // per):
        rows = pl.ds(step * per * srows, per * srows)
        high, low = xh[rows, :], xl[rows, :]
        y = dot(high, mhi_v[...]) + dot(low, mhi_v[...]) + dot(high, mlo_v[...])
        p_s[rows, :] = y[:, 0:C]
        v_s[rows, :] = y[:, C : 2 * C]
        for j in range(per):
            g = step * per + j
            for side in range(2):
                part = y[j * srows : (j + 1) * srows, (2 + side) * C : (3 + side) * C]
                if g == 0:
                    pack[side] = part
                else:
                    pack[side] += pltpu.roll(part, g * SLOT, 1)

    def side_copy(src, dst, send, recv, side):
        return pltpu.make_async_remote_copy(
            src_ref=src.at[side], dst_ref=dst.at[side], send_sem=send.at[side], recv_sem=recv.at[side],
            device_id=((left, right)[side], me), device_id_type=MESH,
        )

    halos = [side_copy(pack, pack_in, halo_send, halo_recv, side) for side in range(2)]
    for copy in halos:
        copy.start()

    def forward(c):
        for d in range(1, half):
            direct_in(d, c).wait_recv()
            to_mate(d, c).start()

    carry = jnp.zeros((R, C), F32)
    for d in range(1, levs):
        total_copy(d).wait_recv()
        owner = (me + levs - d) % levs
        carry = carry + jnp.where(owner > me, tot_in[d - 1], 0.0)
    ch, cl = split(carry)
    yc = dot(ch, mhi_v[0:C, :]) + dot(cl, mhi_v[0:C, :]) + dot(ch, mlo_v[0:C, :])
    cpack[0] = yc[:, 2 * C : 3 * C]
    cpack[1] = yc[:, 3 * C : 4 * C]
    chalos = [side_copy(cpack, cpack_in, chalo_send, chalo_recv, side) for side in range(2)]
    for copy in chalos:
        copy.start()

    for i in (6, 7, 8):
        loads[i].wait()

    def physics(c):
        for d in range(half):
            from_mate(d, c).wait_recv()

        def pair(i, _):
            r = c * CHUNK + 2 * i
            cols = jnp.concatenate([gath[r], gath[r + 1]], axis=1)
            res = dot(w_v[...].reshape(S * L, levs * L), cols)
            for j in range(2):
                mine = res[:, j * C : (j + 1) * C]
                scheme = jnp.broadcast_to(clos_v[pl.ds(r + j, 1), :], (L, C))
                on = jnp.broadcast_to(trig_v[pl.ds(r + j, 1), :].astype(F32), (L, C))
                chosen = mine[0:L]
                for s in range(1, S - 1):
                    chosen = jnp.where(scheme == s, mine[s * L : (s + 1) * L], chosen)
                heat[pl.ds(r + j, L, stride=R), :] = mine[(S - 1) * L :] + on * chosen
            return 0

        lax.fori_loop(0, CHUNK // 2, pair, 0, unroll=True)

    houts = []

    def emit(o):
        def one(k, _):
            hout[k, pl.ds(o * PACK, PACK), :] = heat[pl.ds(pl.multiple_of(k * R + o * PACK, PACK), PACK), :].astype(BF16)
            return 0

        lax.fori_loop(0, L, one, 0, unroll=8)
        rows = pl.ds(o * PACK, PACK)
        copy = pltpu.make_async_copy(hout.at[:, rows, :], h_out.at[:, rows, :], hout_sem.at[o])
        copy.start()
        houts.append(copy)

    outs = []

    def finish():
        lane = lax.broadcasted_iota(jnp.int32, (R, C), 1)
        for side in range(2):
            halos[side].wait_recv()
            chalos[side].wait_recv()

        def edges(to_left, to_right, start, rows):
            at = lax.broadcasted_iota(jnp.int32, (rows, C), 1)
            first = pltpu.roll(to_right, (C - start) % C, 1)
            last = pltpu.roll(to_left, (2 * C - H - start) % C, 1)
            return jnp.where(at < H, first, jnp.where(at >= C - H, last, 0.0))

        p_c = yc[:, 0:C] + edges(cpack_in[0], cpack_in[1], 0, R)
        v_c = yc[:, C : 2 * C] + edges(cpack_in[0], cpack_in[1], H, R)
        for g in range(slots):
            rows = pl.ds(g * srows, srows)
            for field, (held, common) in enumerate(((p_s, p_c), (v_s, v_c))):
                fix = edges(pack_in[0], pack_in[1], g * SLOT + field * H, srows)
                many = held[rows, :] + fix
                held[rows, :] = (many.reshape(srows // R, R, C) + common[None]).reshape(srows, C)
                copy = pltpu.make_async_copy(
                    held.at[rows, :], (p_out, v_out)[field].at[rows, :], out_sem.at[field, g]
                )
                copy.start()
                outs.append(copy)

    per_pack = PACK // CHUNK
    for c in range(chunks):
        forward(c)
        if c == chunks - 1:
            finish()
        if c >= 1:
            physics(c - 1)
            if c % per_pack == 0:
                emit(c // per_pack - 1)
    physics(chunks - 1)
    emit(chunks // per_pack - 1)

    for c in range(chunks):
        for d in range(1, half):
            direct(d, c).wait_send()
        for d in range(half):
            to_mate(d, c).wait_send()
    for d in range(1, levs):
        total_copy(d).wait_send()
    for copy in halos + chalos:
        copy.wait_send()
    for copy in outs + houts:
        copy.wait()


def shards(levs, tiles, theta, thickness, wind, surface, trigger, closure, closure_weights):
    L, R, C = theta.shape
    S = closure_weights.shape[0]
    half = levs // 2
    chunks = R // CHUNK
    slots = C // SLOT
    srows = L * R // slots
    high, low = substep_operator(C)
    flat = (L * R, C)
    anywhere = pl.BlockSpec(memory_space=pl.ANY)
    vmem, dma = pltpu.VMEM, pltpu.SemaphoreType.DMA
    p, v, h = pl.pallas_call(
        functools.partial(kernel, (levs, tiles, L, R, C, S)),
        out_shape=(
            jax.ShapeDtypeStruct(flat, F32), jax.ShapeDtypeStruct(flat, F32), jax.ShapeDtypeStruct((L, R, C), BF16)
        ),
        in_specs=[anywhere] * 9,
        out_specs=(anywhere,) * 3,
        scratch_shapes=[
            vmem(flat, F32), vmem(flat, F32), vmem(flat, F32),
            vmem((R, C), F32), vmem((R, C), jnp.int32), vmem((R, C), jnp.int32),
            vmem((S, L, levs * L), BF16), vmem((2 * C, 4 * C), BF16), vmem((2 * C, 4 * C), BF16),
            vmem((R, levs * L, C), BF16),
            vmem((L * R, 2 * C), BF16), vmem((L * R, 2 * C), BF16),
            vmem(flat, F32), vmem(flat, F32),
            vmem((2, srows, C), F32), vmem((2, srows, C), F32),
            vmem((R, C), F32), vmem((levs - 1, R, C), F32),
            vmem((2, R, C), F32), vmem((2, R, C), F32),
            vmem(flat, F32), vmem((L, R, C), BF16),
            dma((9,)), dma((2, slots)), dma((R // PACK,)),
            dma((max(half - 1, 1), chunks)), dma((max(half - 1, 1), chunks)), dma((half, chunks)), dma((half, chunks)),
            dma((levs - 1,)), dma((levs - 1,)), dma((2,)), dma((2,)), dma((2,)), dma((2,)),
        ],
        compiler_params=pltpu.CompilerParams(
            collective_id=0, has_side_effects=True, vmem_limit_bytes=24 * 1024 * 1024
        ),
        cost_estimate=pl.CostEstimate(flops=10**9, bytes_accessed=4 * 10**6, transcendentals=0),
    )(
        theta.reshape(flat), thickness.reshape(flat), wind.reshape(flat), surface, trigger, closure, closure_weights,
        jnp.asarray(high), jnp.asarray(low),
    )
    return p.reshape(L, R, C), v.reshape(L, R, C), h


def solution(mesh):
    cells, sheet = P("lev", None, "tile"), P(None, "tile")
    return jax.shard_map(
        functools.partial(shards, mesh.shape["lev"], mesh.shape["tile"]),
        mesh=mesh,
        in_specs=(cells, cells, cells, sheet, sheet, sheet, P()),
        out_specs=(cells, cells, cells),
        check_vma=False,
    )
```

```python
import functools

import jax
import jax.numpy as jnp
import numpy as np
from jax import lax
from jax.experimental import pallas as pl
from jax.experimental.pallas import tpu as pltpu
from jax.sharding import PartitionSpec as P

LEVELS = 128
SUBSTEPS = 6
SLOT = 16
CHUNK = 8
PACK = 16

courant = 0.9
F32 = jnp.float32
BF16 = jnp.bfloat16
MESH = pl.DeviceIdType.MESH


def substep_operator(width):
    halo = SUBSTEPS
    pad = 2 * halo
    pressure = np.zeros((2 * width, width + 2 * pad))
    velocity = np.zeros_like(pressure)
    cells = np.arange(width)
    pressure[cells, pad + cells] = 1.0
    velocity[width + cells, pad + cells] = 1.0
    for substep in range(SUBSTEPS):
        velocity = velocity - courant * (np.roll(pressure, -1, axis=1) - pressure)
        pressure = pressure - courant * (velocity - np.roll(velocity, 1, axis=1))
    spare = np.zeros((2 * width, width - 2 * halo))
    before, after = slice(pad - halo, pad), slice(pad + width, pad + width + halo)
    inside = slice(pad, pad + width)
    whole = np.concatenate(
        [
            pressure[:, inside], velocity[:, inside],
            pressure[:, before], velocity[:, before], spare,
            pressure[:, after], velocity[:, after], spare,
        ],
        axis=1,
    )
    return whole.astype(np.float32)


def split(value):
    high = value.astype(BF16)
    return high, (value - high.astype(F32)).astype(BF16)


def dot(a, b):
    return jnp.dot(a, b, preferred_element_type=F32)


def kernel(
    dims,
    theta, thick, wind, surf, trig, clos, wts, operator,
    p_s, v_s, hout,
    theta_v, thick_v, wind_v, surf_v, trig_v, clos_v, w_v, op_v, mhi_v, mlo_v,
    gath, xh, xl, pack, pack_in, tot, tot_in, cpack, cpack_in, heat,
    in_sem, dir_send, dir_recv, par_send, par_recv,
    tot_send, tot_recv, halo_send, halo_recv, chalo_send, chalo_recv,
):
    levs, tiles, L, R, C, S = dims
    half = levs // 2
    chunks = R // CHUNK
    slots = C // SLOT
    srows = L * R // slots
    H = SUBSTEPS
    me = lax.axis_index("lev")
    here = lax.axis_index("tile")
    mate = me + 1 - 2 * (me % 2)
    right, left = (here + 1) % tiles, (here + tiles - 1) % tiles

    loads = [
        pltpu.make_async_copy(src, dst, in_sem.at[i])
        for i, (src, dst) in enumerate(
            [
                (theta, theta_v), (thick, thick_v), (surf, surf_v), (wind, wind_v), (operator, op_v),
                (wts.at[:, pl.ds(pl.multiple_of(me * L, 16), L), :], w_v), (trig, trig_v), (clos, clos_v),
            ]
        )
    ]
    for copy in loads:
        copy.start()
    barrier = pltpu.get_barrier_semaphore()
    for d in range(1, levs):
        pl.semaphore_signal(barrier, inc=1, device_id=(here, (me + d) % levs), device_id_type=MESH)
    for side in (left, right):
        pl.semaphore_signal(barrier, inc=1, device_id=(side, me), device_id_type=MESH)

    def slot_of(rank):
        return pl.ds(pl.multiple_of(rank * L, 16), L)

    def block_copy(owner, c, send, recv, target):
        block = gath.at[pl.ds(c * CHUNK, CHUNK), slot_of(owner), :]
        return pltpu.make_async_remote_copy(
            src_ref=block, dst_ref=block, send_sem=send, recv_sem=recv, device_id=(here, target), device_id_type=MESH
        )

    def direct(d, c):
        return block_copy(me, c, dir_send.at[d - 1, c], dir_recv.at[d - 1, c], (me + 2 * d) % levs)

    def to_mate(d, c):
        return block_copy((me + levs - 2 * d) % levs, c, par_send.at[d, c], par_recv.at[d, c], mate)

    def direct_in(d, c):
        return block_copy(
            (me + levs - 2 * d) % levs, c, dir_send.at[d - 1, c], dir_recv.at[d - 1, c], (me + 2 * d) % levs
        )

    def from_mate(d, c):
        return block_copy((mate + levs - 2 * d) % levs, c, par_send.at[d, c], par_recv.at[d, c], mate)

    loads[0].wait()
    for c in range(chunks):
        def relayout(i, _, c=c):
            r = c * CHUNK + i
            gath[r, slot_of(me), :] = theta_v[pl.ds(r, L, stride=R), :].astype(BF16)
            return 0

        lax.fori_loop(0, CHUNK, relayout, 0, unroll=True)
        if c == 0:
            pl.semaphore_wait(barrier, levs + 1)
        for d in range(1, half):
            direct(d, c).start()
        to_mate(0, c).start()

    for i in (1, 2, 3):
        loads[i].wait()

    def level(i, total):
        rows = pl.ds(pl.multiple_of((L - 1 - i) * R, R), R)
        thermal = theta_v[rows, :] * thick_v[rows, :] * LEVELS ** (-0.5)
        geopot = surf_v[...] + total + 0.5 * thermal
        xh[rows, 0:C], xl[rows, 0:C] = split(geopot)
        xh[rows, C : 2 * C], xl[rows, C : 2 * C] = split(wind_v[rows, :])
        return total + thermal

    tot[...] = lax.fori_loop(0, L, level, jnp.zeros((R, C), F32), unroll=4)

    def total_copy(d):
        return pltpu.make_async_remote_copy(
            src_ref=tot, dst_ref=tot_in.at[d - 1], send_sem=tot_send.at[d - 1], recv_sem=tot_recv.at[d - 1],
            device_id=(here, (me + d) % levs), device_id_type=MESH,
        )

    for d in range(1, levs):
        total_copy(d).start()

    loads[4].wait()
    mhi_v[...], mlo_v[...] = split(op_v[...])
    per = 2
    for step in range(slots // per):
        rows = pl.ds(step * per * srows, per * srows)
        high, low = xh[rows, :], xl[rows, :]
        y = dot(high, mhi_v[...]) + dot(low, mhi_v[...]) + dot(high, mlo_v[...])
        p_s[rows, :] = y[:, 0:C]
        v_s[rows, :] = y[:, C : 2 * C]
        for j in range(per):
            g = step * per + j
            for side in range(2):
                part = y[j * srows : (j + 1) * srows, (2 + side) * C : (3 + side) * C]
                if g == 0:
                    pack[side] = part
                else:
                    pack[side] += pltpu.roll(part, g * SLOT, 1)

    def side_copy(src, dst, send, recv, side):
        return pltpu.make_async_remote_copy(
            src_ref=src.at[side], dst_ref=dst.at[side], send_sem=send.at[side], recv_sem=recv.at[side],
            device_id=((left, right)[side], me), device_id_type=MESH,
        )

    halos = [side_copy(pack, pack_in, halo_send, halo_recv, side) for side in range(2)]
    for copy in halos:
        copy.start()

    def forward(c):
        for d in range(1, half):
            direct_in(d, c).wait_recv()
            to_mate(d, c).start()

    carry = jnp.zeros((R, C), F32)
    for d in range(1, levs):
        total_copy(d).wait_recv()
        owner = (me + levs - d) % levs
        carry = carry + jnp.where(owner > me, tot_in[d - 1], 0.0)
    ch, cl = split(carry)
    yc = dot(ch, mhi_v[0:C, :]) + dot(cl, mhi_v[0:C, :]) + dot(ch, mlo_v[0:C, :])
    cpack[0] = yc[:, 2 * C : 3 * C]
    cpack[1] = yc[:, 3 * C : 4 * C]
    chalos = [side_copy(cpack, cpack_in, chalo_send, chalo_recv, side) for side in range(2)]
    for copy in chalos:
        copy.start()

    for i in (5, 6, 7):
        loads[i].wait()

    def physics(c):
        for d in range(half):
            from_mate(d, c).wait_recv()

        def pair(i, _):
            r = c * CHUNK + 2 * i
            cols = jnp.concatenate([gath[r], gath[r + 1]], axis=1)
            res = dot(w_v[...].reshape(S * L, levs * L), cols)
            for j in range(2):
                mine = res[:, j * C : (j + 1) * C]
                scheme = jnp.broadcast_to(clos_v[pl.ds(r + j, 1), :], (L, C))
                on = jnp.broadcast_to(trig_v[pl.ds(r + j, 1), :].astype(F32), (L, C))
                chosen = mine[0:L]
                for s in range(1, S - 1):
                    chosen = jnp.where(scheme == s, mine[s * L : (s + 1) * L], chosen)
                heat[pl.ds(r + j, L, stride=R), :] = mine[(S - 1) * L :] + on * chosen
            return 0

        lax.fori_loop(0, CHUNK // 2, pair, 0, unroll=True)

    def emit(o):
        def one(k, _):
            hout[k, pl.ds(o * PACK, PACK), :] = heat[pl.ds(pl.multiple_of(k * R + o * PACK, PACK), PACK), :].astype(BF16)
            return 0

        lax.fori_loop(0, L, one, 0, unroll=8)

    def finish():
        lane = lax.broadcasted_iota(jnp.int32, (R, C), 1)
        for side in range(2):
            halos[side].wait_recv()
            chalos[side].wait_recv()

        def edges(to_left, to_right, start, rows):
            at = lax.broadcasted_iota(jnp.int32, (rows, C), 1)
            first = pltpu.roll(to_right, (C - start) % C, 1)
            last = pltpu.roll(to_left, (2 * C - H - start) % C, 1)
            return jnp.where(at < H, first, jnp.where(at >= C - H, last, 0.0))

        p_c = yc[:, 0:C] + edges(cpack_in[0], cpack_in[1], 0, R)
        v_c = yc[:, C : 2 * C] + edges(cpack_in[0], cpack_in[1], H, R)
        for g in range(slots):
            rows = pl.ds(g * srows, srows)
            for field, (held, common) in enumerate(((p_s, p_c), (v_s, v_c))):
                fix = edges(pack_in[0], pack_in[1], g * SLOT + field * H, srows)
                many = held[rows, :] + fix
                held[rows, :] = (many.reshape(srows // R, R, C) + common[None]).reshape(srows, C)

    per_pack = PACK // CHUNK
    for c in range(chunks):
        forward(c)
        if c >= 1:
            physics(c - 1)
            if c % per_pack == 0:
                emit(c // per_pack - 1)
        if c == chunks - 2:
            finish()
    physics(chunks - 1)
    emit(chunks // per_pack - 1)

    for c in range(chunks):
        for d in range(1, half):
            direct(d, c).wait_send()
        for d in range(half):
            to_mate(d, c).wait_send()
    for d in range(1, levs):
        total_copy(d).wait_send()
    for copy in halos + chalos:
        copy.wait_send()


def store_kernel(p, v, h, p_out, v_out, h_out, sem):
    copies = [
        pltpu.make_async_copy(src, dst, sem.at[i]) for i, (src, dst) in enumerate(((p, p_out), (v, v_out), (h, h_out)))
    ]
    for copy in copies:
        copy.start()
    for copy in copies:
        copy.wait()


def shards(levs, tiles, theta, thickness, wind, surface, trigger, closure, closure_weights):
    L, R, C = theta.shape
    S = closure_weights.shape[0]
    half = levs // 2
    chunks = R // CHUNK
    slots = C // SLOT
    srows = L * R // slots
    flat = (L * R, C)
    hbm = pl.BlockSpec(memory_space=pltpu.HBM)
    vmem, dma = pltpu.VMEM, pltpu.SemaphoreType.DMA
    p, v, h = pl.pallas_call(
        functools.partial(kernel, (levs, tiles, L, R, C, S)),
        out_shape=(
            jax.ShapeDtypeStruct(flat, F32), jax.ShapeDtypeStruct(flat, F32), jax.ShapeDtypeStruct((L, R, C), BF16)
        ),
        in_specs=[hbm] * 8,
        out_specs=(pl.BlockSpec(memory_space=pltpu.VMEM),) * 3,
        scratch_shapes=[
            vmem(flat, F32), vmem(flat, F32), vmem(flat, F32),
            vmem((R, C), F32), vmem((R, C), jnp.int32), vmem((R, C), jnp.int32),
            vmem((S, L, levs * L), BF16), vmem((2 * C, 4 * C), F32), vmem((2 * C, 4 * C), BF16), vmem((2 * C, 4 * C), BF16),
            vmem((R, levs * L, C), BF16),
            vmem((L * R, 2 * C), BF16), vmem((L * R, 2 * C), BF16),
            vmem((2, srows, C), F32), vmem((2, srows, C), F32),
            vmem((R, C), F32), vmem((levs - 1, R, C), F32),
            vmem((2, R, C), F32), vmem((2, R, C), F32),
            vmem(flat, F32),
            dma((8,)),
            dma((max(half - 1, 1), chunks)), dma((max(half - 1, 1), chunks)), dma((half, chunks)), dma((half, chunks)),
            dma((levs - 1,)), dma((levs - 1,)), dma((2,)), dma((2,)), dma((2,)), dma((2,)),
        ],
        compiler_params=pltpu.CompilerParams(
            collective_id=0, has_side_effects=True, vmem_limit_bytes=24 * 1024 * 1024
        ),
        cost_estimate=pl.CostEstimate(flops=10**9, bytes_accessed=4 * 10**6, transcendentals=0),
    )(
        *(
            pltpu.with_memory_space_constraint(value, pltpu.HBM)
            for value in (
                theta.reshape(flat), thickness.reshape(flat), wind.reshape(flat), surface, trigger, closure,
                closure_weights, jnp.asarray(substep_operator(C)),
            )
        )
    )
    p, v, h = pl.pallas_call(
        store_kernel,
        out_shape=tuple(jax.ShapeDtypeStruct(a.shape, a.dtype) for a in (p, v, h)),
        in_specs=[pl.BlockSpec(memory_space=pltpu.VMEM)] * 3,
        out_specs=(hbm,) * 3,
        scratch_shapes=[dma((3,))],
    )(p, v, h)
    return p.reshape(L, R, C), v.reshape(L, R, C), h


def solution(mesh):
    cells, sheet = P("lev", None, "tile"), P(None, "tile")
    return jax.shard_map(
        functools.partial(shards, mesh.shape["lev"], mesh.shape["tile"]),
        mesh=mesh,
        in_specs=(cells, cells, cells, sheet, sheet, sheet, P()),
        out_specs=(cells, cells, cells),
        check_vma=False,
    )
```

```python
import functools

import jax
import jax.numpy as jnp
import numpy as np
from jax import lax
from jax.experimental import pallas as pl
from jax.experimental.pallas import tpu as pltpu
from jax.sharding import PartitionSpec as P

LEVELS = 128
SUBSTEPS = 6
SLOT = 16
CHUNK = 8
PACK = 16

courant = 0.9
F32 = jnp.float32
BF16 = jnp.bfloat16
MESH = pl.DeviceIdType.MESH


def substep_operator(width):
    halo = SUBSTEPS
    pad = 2 * halo
    pressure = np.zeros((2 * width, width + 2 * pad))
    velocity = np.zeros_like(pressure)
    cells = np.arange(width)
    pressure[cells, pad + cells] = 1.0
    velocity[width + cells, pad + cells] = 1.0
    for substep in range(SUBSTEPS):
        velocity = velocity - courant * (np.roll(pressure, -1, axis=1) - pressure)
        pressure = pressure - courant * (velocity - np.roll(velocity, 1, axis=1))
    spare = np.zeros((2 * width, width - 2 * halo))
    before, after = slice(pad - halo, pad), slice(pad + width, pad + width + halo)
    inside = slice(pad, pad + width)
    whole = np.concatenate(
        [
            pressure[:, inside], velocity[:, inside],
            pressure[:, before], velocity[:, before], spare,
            pressure[:, after], velocity[:, after], spare,
        ],
        axis=1,
    )
    return whole.astype(np.float32)


def split(value):
    high = value.astype(BF16)
    return high, (value - high.astype(F32)).astype(BF16)


def dot(a, b):
    return jnp.dot(a, b, preferred_element_type=F32)


def kernel(
    dims,
    theta, thick, wind, surf, trig, clos, wts, operator,
    p_s, v_s, heat, pack_in, cmain, cpack_in,
    theta_v, thick_v, wind_v, surf_v, trig_v, clos_v, w_v, op_v, mhi_v, mlo_v,
    gath, xh, xl, pack, tot, tot_in, cpack,
    in_sem, dir_send, dir_recv, par_send, par_recv,
    tot_send, tot_recv, halo_send, halo_recv, chalo_send, chalo_recv,
):
    levs, tiles, L, R, C, S = dims
    half = levs // 2
    chunks = R // CHUNK
    slots = C // SLOT
    srows = L * R // slots
    H = SUBSTEPS
    me = lax.axis_index("lev")
    here = lax.axis_index("tile")
    mate = me + 1 - 2 * (me % 2)
    right, left = (here + 1) % tiles, (here + tiles - 1) % tiles

    loads = [
        pltpu.make_async_copy(src, dst, in_sem.at[i])
        for i, (src, dst) in enumerate(
            [
                (theta, theta_v), (thick, thick_v), (surf, surf_v), (wind, wind_v), (operator, op_v),
                (wts.at[:, pl.ds(pl.multiple_of(me * L, 16), L), :], w_v), (trig, trig_v), (clos, clos_v),
            ]
        )
    ]
    for copy in loads:
        copy.start()
    barrier = pltpu.get_barrier_semaphore()
    for d in range(1, levs):
        pl.semaphore_signal(barrier, inc=1, device_id=(here, (me + d) % levs), device_id_type=MESH)
    for side in (left, right):
        pl.semaphore_signal(barrier, inc=1, device_id=(side, me), device_id_type=MESH)

    def slot_of(rank):
        return pl.ds(pl.multiple_of(rank * L, 16), L)

    def block_copy(owner, c, send, recv, target):
        block = gath.at[pl.ds(c * CHUNK, CHUNK), slot_of(owner), :]
        return pltpu.make_async_remote_copy(
            src_ref=block, dst_ref=block, send_sem=send, recv_sem=recv, device_id=(here, target), device_id_type=MESH
        )

    def direct(d, c):
        return block_copy(me, c, dir_send.at[d - 1, c], dir_recv.at[d - 1, c], (me + 2 * d) % levs)

    def to_mate(d, c):
        return block_copy((me + levs - 2 * d) % levs, c, par_send.at[d, c], par_recv.at[d, c], mate)

    def direct_in(d, c):
        return block_copy(
            (me + levs - 2 * d) % levs, c, dir_send.at[d - 1, c], dir_recv.at[d - 1, c], (me + 2 * d) % levs
        )

    def from_mate(d, c):
        return block_copy((mate + levs - 2 * d) % levs, c, par_send.at[d, c], par_recv.at[d, c], mate)

    loads[0].wait()
    for c in range(chunks):
        def relayout(i, _, c=c):
            r = c * CHUNK + i
            gath[r, slot_of(me), :] = theta_v[pl.ds(r, L, stride=R), :].astype(BF16)
            return 0

        lax.fori_loop(0, CHUNK, relayout, 0, unroll=True)
        if c == 0:
            pl.semaphore_wait(barrier, levs + 1)
        for d in range(1, half):
            direct(d, c).start()
        to_mate(0, c).start()

    for i in (1, 2, 3):
        loads[i].wait()

    def level(i, total):
        rows = pl.ds(pl.multiple_of((L - 1 - i) * R, R), R)
        thermal = theta_v[rows, :] * thick_v[rows, :] * LEVELS ** (-0.5)
        geopot = surf_v[...] + total + 0.5 * thermal
        xh[rows, 0:C], xl[rows, 0:C] = split(geopot)
        xh[rows, C : 2 * C], xl[rows, C : 2 * C] = split(wind_v[rows, :])
        return total + thermal

    tot[...] = lax.fori_loop(0, L, level, jnp.zeros((R, C), F32), unroll=4)

    def total_copy(d):
        return pltpu.make_async_remote_copy(
            src_ref=tot, dst_ref=tot_in.at[d - 1], send_sem=tot_send.at[d - 1], recv_sem=tot_recv.at[d - 1],
            device_id=(here, (me + d) % levs), device_id_type=MESH,
        )

    for d in range(1, levs):
        total_copy(d).start()

    loads[4].wait()
    mhi_v[...], mlo_v[...] = split(op_v[...])
    per = 2
    for step in range(slots // per):
        rows = pl.ds(step * per * srows, per * srows)
        high, low = xh[rows, :], xl[rows, :]
        y = dot(high, mhi_v[...]) + dot(low, mhi_v[...]) + dot(high, mlo_v[...])
        p_s[rows, :] = y[:, 0:C]
        v_s[rows, :] = y[:, C : 2 * C]
        for j in range(per):
            g = step * per + j
            for side in range(2):
                part = y[j * srows : (j + 1) * srows, (2 + side) * C : (3 + side) * C]
                if g == 0:
                    pack[side] = part
                else:
                    pack[side] += pltpu.roll(part, g * SLOT, 1)

    def side_copy(src, dst, send, recv, side):
        return pltpu.make_async_remote_copy(
            src_ref=src.at[side], dst_ref=dst.at[side], send_sem=send.at[side], recv_sem=recv.at[side],
            device_id=((left, right)[side], me), device_id_type=MESH,
        )

    halos = [side_copy(pack, pack_in, halo_send, halo_recv, side) for side in range(2)]
    for copy in halos:
        copy.start()

    def forward(c):
        for d in range(1, half):
            direct_in(d, c).wait_recv()
            to_mate(d, c).start()

    carry = jnp.zeros((R, C), F32)
    for d in range(1, levs):
        total_copy(d).wait_recv()
        owner = (me + levs - d) % levs
        carry = carry + jnp.where(owner > me, tot_in[d - 1], 0.0)
    ch, cl = split(carry)
    yc = dot(ch, mhi_v[0:C, :]) + dot(cl, mhi_v[0:C, :]) + dot(ch, mlo_v[0:C, :])
    cmain[0] = yc[:, 0:C]
    cmain[1] = yc[:, C : 2 * C]
    cpack[0] = yc[:, 2 * C : 3 * C]
    cpack[1] = yc[:, 3 * C : 4 * C]
    chalos = [side_copy(cpack, cpack_in, chalo_send, chalo_recv, side) for side in range(2)]
    for copy in chalos:
        copy.start()

    for i in (5, 6, 7):
        loads[i].wait()

    def physics(c):
        for d in range(half):
            from_mate(d, c).wait_recv()

        def pair(i, _):
            r = c * CHUNK + 2 * i
            cols = jnp.concatenate([gath[r], gath[r + 1]], axis=1)
            res = dot(w_v[...].reshape(S * L, levs * L), cols)
            for j in range(2):
                mine = res[:, j * C : (j + 1) * C]
                scheme = jnp.broadcast_to(clos_v[pl.ds(r + j, 1), :], (L, C))
                on = jnp.broadcast_to(trig_v[pl.ds(r + j, 1), :].astype(F32), (L, C))
                chosen = mine[0:L]
                for s in range(1, S - 1):
                    chosen = jnp.where(scheme == s, mine[s * L : (s + 1) * L], chosen)
                heat[pl.ds(r + j, L, stride=R), :] = mine[(S - 1) * L :] + on * chosen
            return 0

        lax.fori_loop(0, CHUNK // 2, pair, 0, unroll=True)

    for c in range(chunks):
        forward(c)
        if c >= 1:
            physics(c - 1)
    physics(chunks - 1)

    for copy in halos + chalos:
        copy.wait_recv()
    for c in range(chunks):
        for d in range(1, half):
            direct(d, c).wait_send()
        for d in range(half):
            to_mate(d, c).wait_send()
    for d in range(1, levs):
        total_copy(d).wait_send()
    for copy in halos + chalos:
        copy.wait_send()


def finish_kernel(p_s, v_s, heat, pack, cmain, cpack, p_out, v_out, h_out, done, hout, out_sem, hout_sem):
    L, R, C = hout.shape
    slots = C // SLOT
    srows = L * R // slots
    H = SUBSTEPS
    copies = []

    def emit(o):
        rows = pl.ds(o * PACK, PACK)

        def one(k, _):
            hout[k, rows, :] = heat[pl.ds(pl.multiple_of(k * R + o * PACK, PACK), PACK), :].astype(BF16)
            return 0

        lax.fori_loop(0, L, one, 0, unroll=8)
        copy = pltpu.make_async_copy(hout.at[:, rows, :], h_out.at[:, rows, :], hout_sem.at[o])
        copy.start()
        copies.append(copy)

    def edges(to_left, to_right, start, rows):
        at = lax.broadcasted_iota(jnp.int32, (rows, C), 1)
        first = pltpu.roll(to_right, (C - start) % C, 1)
        last = pltpu.roll(to_left, (2 * C - H - start) % C, 1)
        return jnp.where(at < H, first, jnp.where(at >= C - H, last, 0.0))

    for o in range(R // PACK):
        emit(o)
    common = [cmain[field] + edges(cpack[0], cpack[1], field * H, R) for field in range(2)]
    for g in range(slots):
        rows = pl.ds(g * srows, srows)
        for field, (held, out) in enumerate(((p_s, p_out), (v_s, v_out))):
            fix = edges(pack[0], pack[1], g * SLOT + field * H, srows)
            many = (held[rows, :] + fix).reshape(srows // R, R, C) + common[field][None]
            done[field, rows, :] = many.reshape(srows, C)
            copy = pltpu.make_async_copy(done.at[field, rows, :], out.at[rows, :], out_sem.at[field, g])
            copy.start()
            copies.append(copy)
    for copy in copies:
        copy.wait()


def shards(levs, tiles, theta, thickness, wind, surface, trigger, closure, closure_weights):
    L, R, C = theta.shape
    S = closure_weights.shape[0]
    half = levs // 2
    chunks = R // CHUNK
    slots = C // SLOT
    srows = L * R // slots
    flat = (L * R, C)
    near = pl.BlockSpec(memory_space=pltpu.VMEM)
    hbm = pl.BlockSpec(memory_space=pltpu.HBM)
    vmem, dma = pltpu.VMEM, pltpu.SemaphoreType.DMA
    parts = pl.pallas_call(
        functools.partial(kernel, (levs, tiles, L, R, C, S)),
        out_shape=(
            vmem(flat, F32), vmem(flat, F32), vmem(flat, F32),
            vmem((2, srows, C), F32), vmem((2, R, C), F32), vmem((2, R, C), F32),
        ),
        in_specs=[hbm] * 8,
        out_specs=(near,) * 6,
        scratch_shapes=[
            vmem(flat, F32), vmem(flat, F32), vmem(flat, F32),
            vmem((R, C), F32), vmem((R, C), jnp.int32), vmem((R, C), jnp.int32),
            vmem((S, L, levs * L), BF16), vmem((2 * C, 4 * C), F32), vmem((2 * C, 4 * C), BF16), vmem((2 * C, 4 * C), BF16),
            vmem((R, levs * L, C), BF16),
            vmem((L * R, 2 * C), BF16), vmem((L * R, 2 * C), BF16),
            vmem((2, srows, C), F32),
            vmem((R, C), F32), vmem((levs - 1, R, C), F32),
            vmem((2, R, C), F32),
            dma((8,)),
            dma((max(half - 1, 1), chunks)), dma((max(half - 1, 1), chunks)), dma((half, chunks)), dma((half, chunks)),
            dma((levs - 1,)), dma((levs - 1,)), dma((2,)), dma((2,)), dma((2,)), dma((2,)),
        ],
        compiler_params=pltpu.CompilerParams(
            collective_id=0, has_side_effects=True, vmem_limit_bytes=24 * 1024 * 1024
        ),
        cost_estimate=pl.CostEstimate(flops=10**9, bytes_accessed=4 * 10**6, transcendentals=0),
    )(
        *(
            pltpu.with_memory_space_constraint(value, pltpu.HBM)
            for value in (
                theta.reshape(flat), thickness.reshape(flat), wind.reshape(flat), surface, trigger, closure,
                closure_weights, jnp.asarray(substep_operator(C)),
            )
        )
    )
    p, v, h = pl.pallas_call(
        finish_kernel,
        out_shape=(
            jax.ShapeDtypeStruct(flat, F32), jax.ShapeDtypeStruct(flat, F32), jax.ShapeDtypeStruct((L, R, C), BF16)
        ),
        in_specs=[near] * 6,
        out_specs=(hbm,) * 3,
        scratch_shapes=[
            vmem((2,) + flat, F32), vmem((L, R, C), BF16), dma((2, slots)), dma((R // PACK,)),
        ],
        compiler_params=pltpu.CompilerParams(vmem_limit_bytes=16 * 1024 * 1024),
        cost_estimate=pl.CostEstimate(flops=10**6, bytes_accessed=3 * 10**6, transcendentals=0),
    )(*(pltpu.with_memory_space_constraint(part, pltpu.VMEM) for part in parts))
    return p.reshape(L, R, C), v.reshape(L, R, C), h


def solution(mesh):
    cells, sheet = P("lev", None, "tile"), P(None, "tile")
    return jax.shard_map(
        functools.partial(shards, mesh.shape["lev"], mesh.shape["tile"]),
        mesh=mesh,
        in_specs=(cells, cells, cells, sheet, sheet, sheet, P()),
        out_specs=(cells, cells, cells),
        check_vma=False,
    )
```

```python
import functools

import jax
import jax.numpy as jnp
import numpy as np
from jax import lax
from jax.experimental import pallas as pl
from jax.experimental.pallas import tpu as pltpu
from jax.sharding import PartitionSpec as P

LEVELS = 128
SUBSTEPS = 6
SLOT = 16
CHUNK = 8
PACK = 16

courant = 0.9
F32 = jnp.float32
BF16 = jnp.bfloat16
MESH = pl.DeviceIdType.MESH


def substep_operator(width):
    halo = SUBSTEPS
    pad = 2 * halo
    pressure = np.zeros((2 * width, width + 2 * pad))
    velocity = np.zeros_like(pressure)
    cells = np.arange(width)
    pressure[cells, pad + cells] = 1.0
    velocity[width + cells, pad + cells] = 1.0
    for substep in range(SUBSTEPS):
        velocity = velocity - courant * (np.roll(pressure, -1, axis=1) - pressure)
        pressure = pressure - courant * (velocity - np.roll(velocity, 1, axis=1))
    spare = np.zeros((2 * width, width - 2 * halo))
    before, after = slice(pad - halo, pad), slice(pad + width, pad + width + halo)
    inside = slice(pad, pad + width)
    whole = np.concatenate(
        [
            pressure[:, inside], velocity[:, inside],
            pressure[:, before], velocity[:, before], spare,
            pressure[:, after], velocity[:, after], spare,
        ],
        axis=1,
    )
    return whole.astype(np.float32)


def split(value):
    high = value.astype(BF16)
    return high, (value - high.astype(F32)).astype(BF16)


def dot(a, b):
    return jnp.dot(a, b, preferred_element_type=F32)


def kernel(
    dims,
    theta, thick, wind, surf, trig, clos, wts, operator,
    p_s, v_s, heat, pack_in, cmain, cpack_in,
    theta_v, thick_v, wind_v, surf_v, trig_v, clos_v, w_v, op_v, mhi_v, mlo_v,
    gath, xh, xl, pack, tot, cpack,
    in_sem, dir_send, dir_recv, par_send, par_recv,
    tot_send, tot_recv, totm_send, totm_recv, halo_send, halo_recv, chalo_send, chalo_recv,
):
    levs, tiles, L, R, C, S = dims
    half = levs // 2
    chunks = R // CHUNK
    slots = C // SLOT
    srows = L * R // slots
    H = SUBSTEPS
    me = lax.axis_index("lev")
    here = lax.axis_index("tile")
    mate = me + 1 - 2 * (me % 2)
    right, left = (here + 1) % tiles, (here + tiles - 1) % tiles

    loads = [
        pltpu.make_async_copy(src, dst, in_sem.at[i])
        for i, (src, dst) in enumerate(
            [
                (theta, theta_v), (thick, thick_v), (surf, surf_v), (wind, wind_v), (operator, op_v),
                (wts.at[:, pl.ds(pl.multiple_of(me * L, 16), L), :], w_v), (trig, trig_v), (clos, clos_v),
            ]
        )
    ]
    for copy in loads:
        copy.start()
    barrier = pltpu.get_barrier_semaphore()
    for d in range(1, levs):
        pl.semaphore_signal(barrier, inc=1, device_id=(here, (me + d) % levs), device_id_type=MESH)
    for side in (left, right):
        pl.semaphore_signal(barrier, inc=1, device_id=(side, me), device_id_type=MESH)

    def slot_of(rank):
        return pl.ds(pl.multiple_of(rank * L, 16), L)

    def block_copy(owner, c, send, recv, target):
        block = gath.at[pl.ds(c * CHUNK, CHUNK), slot_of(owner), :]
        return pltpu.make_async_remote_copy(
            src_ref=block, dst_ref=block, send_sem=send, recv_sem=recv, device_id=(here, target), device_id_type=MESH
        )

    def direct(d, c):
        return block_copy(me, c, dir_send.at[d - 1, c], dir_recv.at[d - 1, c], (me + 2 * d) % levs)

    def to_mate(d, c):
        return block_copy((me + levs - 2 * d) % levs, c, par_send.at[d, c], par_recv.at[d, c], mate)

    def direct_in(d, c):
        return block_copy(
            (me + levs - 2 * d) % levs, c, dir_send.at[d - 1, c], dir_recv.at[d - 1, c], (me + 2 * d) % levs
        )

    def from_mate(d, c):
        return block_copy((mate + levs - 2 * d) % levs, c, par_send.at[d, c], par_recv.at[d, c], mate)

    def total_copy(owner, send, recv, target):
        return pltpu.make_async_remote_copy(
            src_ref=tot.at[owner], dst_ref=tot.at[owner], send_sem=send, recv_sem=recv,
            device_id=(here, target), device_id_type=MESH,
        )

    def total_direct(d, inward=False):
        owner = (me + levs - 2 * d) % levs if inward else me
        return total_copy(owner, tot_send.at[d - 1], tot_recv.at[d - 1], (me + 2 * d) % levs)

    def total_mate(d, inward=False):
        owner = ((mate if inward else me) + levs - 2 * d) % levs
        return total_copy(owner, totm_send.at[d], totm_recv.at[d], mate)

    loads[0].wait()
    loads[1].wait()

    def column(i, total):
        rows = pl.ds(pl.multiple_of((L - 1 - i) * R, R), R)
        return total + theta_v[rows, :] * thick_v[rows, :] * LEVELS ** (-0.5)

    tot[me] = lax.fori_loop(0, L, column, jnp.zeros((R, C), F32), unroll=8)

    for c in range(chunks):
        def relayout(i, _, c=c):
            r = c * CHUNK + i
            gath[r, slot_of(me), :] = theta_v[pl.ds(r, L, stride=R), :].astype(BF16)
            return 0

        lax.fori_loop(0, CHUNK, relayout, 0, unroll=True)
        if c == 0:
            pl.semaphore_wait(barrier, levs + 1)
            for d in range(1, half):
                total_direct(d).start()
            total_mate(0).start()
        for d in range(1, half):
            direct(d, c).start()
        to_mate(0, c).start()

    for i in (2, 3):
        loads[i].wait()

    def level(i, total):
        rows = pl.ds(pl.multiple_of((L - 1 - i) * R, R), R)
        thermal = theta_v[rows, :] * thick_v[rows, :] * LEVELS ** (-0.5)
        geopot = surf_v[...] + total + 0.5 * thermal
        xh[rows, 0:C], xl[rows, 0:C] = split(geopot)
        xh[rows, C : 2 * C], xl[rows, C : 2 * C] = split(wind_v[rows, :])
        return total + thermal

    lax.fori_loop(0, L, level, jnp.zeros((R, C), F32), unroll=4)

    loads[4].wait()
    mhi_v[...], mlo_v[...] = split(op_v[...])
    per = 2
    for step in range(slots // per):
        if step == slots // per // 2:
            for d in range(1, half):
                total_direct(d, True).wait_recv()
                total_mate(d).start()
        rows = pl.ds(step * per * srows, per * srows)
        high, low = xh[rows, :], xl[rows, :]
        y = dot(high, mhi_v[...]) + dot(low, mhi_v[...]) + dot(high, mlo_v[...])
        p_s[rows, :] = y[:, 0:C]
        v_s[rows, :] = y[:, C : 2 * C]
        for j in range(per):
            g = step * per + j
            for side in range(2):
                part = y[j * srows : (j + 1) * srows, (2 + side) * C : (3 + side) * C]
                if g == 0:
                    pack[side] = part
                else:
                    pack[side] += pltpu.roll(part, g * SLOT, 1)

    def side_copy(src, dst, send, recv, side):
        return pltpu.make_async_remote_copy(
            src_ref=src.at[side], dst_ref=dst.at[side], send_sem=send.at[side], recv_sem=recv.at[side],
            device_id=((left, right)[side], me), device_id_type=MESH,
        )

    halos = [side_copy(pack, pack_in, halo_send, halo_recv, side) for side in range(2)]
    for copy in halos:
        copy.start()

    def forward(c):
        for d in range(1, half):
            direct_in(d, c).wait_recv()
            to_mate(d, c).start()

    forward(0)
    for d in range(half):
        total_mate(d, True).wait_recv()
    carry = jnp.zeros((R, C), F32)
    for owner in range(levs):
        carry = carry + jnp.where(owner > me, tot[owner], 0.0)
    ch, cl = split(carry)
    yc = dot(ch, mhi_v[0:C, :]) + dot(cl, mhi_v[0:C, :]) + dot(ch, mlo_v[0:C, :])
    cmain[0] = yc[:, 0:C]
    cmain[1] = yc[:, C : 2 * C]
    cpack[0] = yc[:, 2 * C : 3 * C]
    cpack[1] = yc[:, 3 * C : 4 * C]
    chalos = [side_copy(cpack, cpack_in, chalo_send, chalo_recv, side) for side in range(2)]
    for copy in chalos:
        copy.start()

    for i in (5, 6, 7):
        loads[i].wait()

    def physics(c):
        for d in range(half):
            from_mate(d, c).wait_recv()

        def pair(i, _):
            r = c * CHUNK + 2 * i
            cols = jnp.concatenate([gath[r], gath[r + 1]], axis=1)
            res = dot(w_v[...].reshape(S * L, levs * L), cols)
            for j in range(2):
                mine = res[:, j * C : (j + 1) * C]
                scheme = jnp.broadcast_to(clos_v[pl.ds(r + j, 1), :], (L, C))
                on = jnp.broadcast_to(trig_v[pl.ds(r + j, 1), :].astype(F32), (L, C))
                chosen = mine[0:L]
                for s in range(1, S - 1):
                    chosen = jnp.where(scheme == s, mine[s * L : (s + 1) * L], chosen)
                heat[pl.ds(r + j, L, stride=R), :] = mine[(S - 1) * L :] + on * chosen
            return 0

        lax.fori_loop(0, CHUNK // 2, pair, 0, unroll=True)

    for c in range(1, chunks):
        forward(c)
        physics(c - 1)
    physics(chunks - 1)

    for copy in halos + chalos:
        copy.wait_recv()
    for c in range(chunks):
        for d in range(1, half):
            direct(d, c).wait_send()
        for d in range(half):
            to_mate(d, c).wait_send()
    for d in range(1, half):
        total_direct(d).wait_send()
    for d in range(half):
        total_mate(d).wait_send()
    for copy in halos + chalos:
        copy.wait_send()


def finish_kernel(p_s, v_s, heat, pack, cmain, cpack, p_out, v_out, h_out, done, hout, out_sem, hout_sem):
    L, R, C = hout.shape
    slots = C // SLOT
    srows = L * R // slots
    H = SUBSTEPS
    copies = []

    def emit(o):
        rows = pl.ds(o * PACK, PACK)

        def one(k, _):
            hout[k, rows, :] = heat[pl.ds(pl.multiple_of(k * R + o * PACK, PACK), PACK), :].astype(BF16)
            return 0

        lax.fori_loop(0, L, one, 0, unroll=8)
        copy = pltpu.make_async_copy(hout.at[:, rows, :], h_out.at[:, rows, :], hout_sem.at[o])
        copy.start()
        copies.append(copy)

    def edges(to_left, to_right, start, rows):
        at = lax.broadcasted_iota(jnp.int32, (rows, C), 1)
        first = pltpu.roll(to_right, (C - start) % C, 1)
        last = pltpu.roll(to_left, (2 * C - H - start) % C, 1)
        return jnp.where(at < H, first, jnp.where(at >= C - H, last, 0.0))

    for o in range(R // PACK):
        emit(o)
    common = [cmain[field] + edges(cpack[0], cpack[1], field * H, R) for field in range(2)]
    for g in range(slots):
        rows = pl.ds(g * srows, srows)
        for field, (held, out) in enumerate(((p_s, p_out), (v_s, v_out))):
            fix = edges(pack[0], pack[1], g * SLOT + field * H, srows)
            many = (held[rows, :] + fix).reshape(srows // R, R, C) + common[field][None]
            done[field, rows, :] = many.reshape(srows, C)
            copy = pltpu.make_async_copy(done.at[field, rows, :], out.at[rows, :], out_sem.at[field, g])
            copy.start()
            copies.append(copy)
    for copy in copies:
        copy.wait()


def shards(levs, tiles, theta, thickness, wind, surface, trigger, closure, closure_weights):
    L, R, C = theta.shape
    S = closure_weights.shape[0]
    half = levs // 2
    chunks = R // CHUNK
    slots = C // SLOT
    srows = L * R // slots
    flat = (L * R, C)
    near = pl.BlockSpec(memory_space=pltpu.VMEM)
    hbm = pl.BlockSpec(memory_space=pltpu.HBM)
    vmem, dma = pltpu.VMEM, pltpu.SemaphoreType.DMA
    parts = pl.pallas_call(
        functools.partial(kernel, (levs, tiles, L, R, C, S)),
        out_shape=(
            vmem(flat, F32), vmem(flat, F32), vmem(flat, F32),
            vmem((2, srows, C), F32), vmem((2, R, C), F32), vmem((2, R, C), F32),
        ),
        in_specs=[hbm] * 8,
        out_specs=(near,) * 6,
        scratch_shapes=[
            vmem(flat, F32), vmem(flat, F32), vmem(flat, F32),
            vmem((R, C), F32), vmem((R, C), jnp.int32), vmem((R, C), jnp.int32),
            vmem((S, L, levs * L), BF16), vmem((2 * C, 4 * C), F32), vmem((2 * C, 4 * C), BF16), vmem((2 * C, 4 * C), BF16),
            vmem((R, levs * L, C), BF16),
            vmem((L * R, 2 * C), BF16), vmem((L * R, 2 * C), BF16),
            vmem((2, srows, C), F32),
            vmem((levs, R, C), F32),
            vmem((2, R, C), F32),
            dma((8,)),
            dma((max(half - 1, 1), chunks)), dma((max(half - 1, 1), chunks)), dma((half, chunks)), dma((half, chunks)),
            dma((max(half - 1, 1),)), dma((max(half - 1, 1),)), dma((half,)), dma((half,)), dma((2,)), dma((2,)), dma((2,)), dma((2,)),
        ],
        compiler_params=pltpu.CompilerParams(
            collective_id=0, has_side_effects=True, vmem_limit_bytes=24 * 1024 * 1024
        ),
        cost_estimate=pl.CostEstimate(flops=10**9, bytes_accessed=4 * 10**6, transcendentals=0),
    )(
        *(
            pltpu.with_memory_space_constraint(value, pltpu.HBM)
            for value in (
                theta.reshape(flat), thickness.reshape(flat), wind.reshape(flat), surface, trigger, closure,
                closure_weights, jnp.asarray(substep_operator(C)),
            )
        )
    )
    p, v, h = pl.pallas_call(
        finish_kernel,
        out_shape=(
            jax.ShapeDtypeStruct(flat, F32), jax.ShapeDtypeStruct(flat, F32), jax.ShapeDtypeStruct((L, R, C), BF16)
        ),
        in_specs=[near] * 6,
        out_specs=(hbm,) * 3,
        scratch_shapes=[
            vmem((2,) + flat, F32), vmem((L, R, C), BF16), dma((2, slots)), dma((R // PACK,)),
        ],
        compiler_params=pltpu.CompilerParams(vmem_limit_bytes=16 * 1024 * 1024),
        cost_estimate=pl.CostEstimate(flops=10**6, bytes_accessed=3 * 10**6, transcendentals=0),
    )(*(pltpu.with_memory_space_constraint(part, pltpu.VMEM) for part in parts))
    return p.reshape(L, R, C), v.reshape(L, R, C), h


def solution(mesh):
    cells, sheet = P("lev", None, "tile"), P(None, "tile")
    return jax.shard_map(
        functools.partial(shards, mesh.shape["lev"], mesh.shape["tile"]),
        mesh=mesh,
        in_specs=(cells, cells, cells, sheet, sheet, sheet, P()),
        out_specs=(cells, cells, cells),
        check_vma=False,
    )
```

```python
import functools

import jax
import jax.numpy as jnp
import numpy as np
from jax import lax
from jax.experimental import pallas as pl
from jax.experimental.pallas import tpu as pltpu
from jax.sharding import PartitionSpec as P

LEVELS = 128
SUBSTEPS = 6
SLOT = 16
CHUNK = 8
PACK = 16

courant = 0.9
F32 = jnp.float32
BF16 = jnp.bfloat16
MESH = pl.DeviceIdType.MESH


def substep_operator(width):
    halo = SUBSTEPS
    pad = 2 * halo
    pressure = np.zeros((2 * width, width + 2 * pad))
    velocity = np.zeros_like(pressure)
    cells = np.arange(width)
    pressure[cells, pad + cells] = 1.0
    velocity[width + cells, pad + cells] = 1.0
    for substep in range(SUBSTEPS):
        velocity = velocity - courant * (np.roll(pressure, -1, axis=1) - pressure)
        pressure = pressure - courant * (velocity - np.roll(velocity, 1, axis=1))
    spare = np.zeros((2 * width, width - 2 * halo))
    before, after = slice(pad - halo, pad), slice(pad + width, pad + width + halo)
    inside = slice(pad, pad + width)
    whole = np.concatenate(
        [
            pressure[:, inside], velocity[:, inside],
            pressure[:, before], velocity[:, before], spare,
            pressure[:, after], velocity[:, after], spare,
        ],
        axis=1,
    )
    return whole.astype(np.float32)


def split(value):
    high = value.astype(BF16)
    return high, (value - high.astype(F32)).astype(BF16)


def dot(a, b):
    return jnp.dot(a, b, preferred_element_type=F32)


def kernel(
    dims,
    theta, thick, wind, surf, trig, clos, wts, operator,
    p_s, v_s, heat,
    theta_3d, thick_v, wind_v, surf_v, trig_v, clos_v, w_v, op_v, mhi_v, mlo_v,
    gath, xh, xl, pack, pack_in, tot, cpack, cpack_in,
    theta_sem, in_sem, dir_send, dir_recv, par_send, par_recv,
    tot_send, tot_recv, totm_send, totm_recv, halo_send, halo_recv, chalo_send, chalo_recv,
):
    levs, tiles, L, R, C, S = dims
    half = levs // 2
    chunks = R // CHUNK
    slots = C // SLOT
    srows = L * R // slots
    H = SUBSTEPS
    me = lax.axis_index("lev")
    here = lax.axis_index("tile")
    mate = me + 1 - 2 * (me % 2)
    theta_v = theta_3d.reshape(L * R, C)
    right, left = (here + 1) % tiles, (here + tiles - 1) % tiles

    loads = [
        pltpu.make_async_copy(src, dst, in_sem.at[i])
        for i, (src, dst) in enumerate(
            [
                (thick, thick_v), (surf, surf_v), (wind, wind_v), (operator, op_v),
                (wts.at[:, pl.ds(pl.multiple_of(me * L, 16), L), :], w_v), (trig, trig_v), (clos, clos_v),
            ]
        )
    ]
    theta_loads = [
        pltpu.make_async_copy(
            theta.at[:, pl.ds(c * CHUNK, CHUNK), :], theta_3d.at[:, pl.ds(c * CHUNK, CHUNK), :], theta_sem.at[c]
        )
        for c in range(chunks)
    ]
    for copy in theta_loads + loads:
        copy.start()
    barrier = pltpu.get_barrier_semaphore()
    for d in range(1, levs):
        pl.semaphore_signal(barrier, inc=1, device_id=(here, (me + d) % levs), device_id_type=MESH)
    for side in (left, right):
        pl.semaphore_signal(barrier, inc=1, device_id=(side, me), device_id_type=MESH)

    def slot_of(rank):
        return pl.ds(pl.multiple_of(rank * L, 16), L)

    def block_copy(owner, c, send, recv, target):
        block = gath.at[pl.ds(c * CHUNK, CHUNK), slot_of(owner), :]
        return pltpu.make_async_remote_copy(
            src_ref=block, dst_ref=block, send_sem=send, recv_sem=recv, device_id=(here, target), device_id_type=MESH
        )

    def direct(d, c):
        return block_copy(me, c, dir_send.at[d - 1, c], dir_recv.at[d - 1, c], (me + 2 * d) % levs)

    def to_mate(d, c):
        return block_copy((me + levs - 2 * d) % levs, c, par_send.at[d, c], par_recv.at[d, c], mate)

    def direct_in(d, c):
        return block_copy(
            (me + levs - 2 * d) % levs, c, dir_send.at[d - 1, c], dir_recv.at[d - 1, c], (me + 2 * d) % levs
        )

    def from_mate(d, c):
        return block_copy((mate + levs - 2 * d) % levs, c, par_send.at[d, c], par_recv.at[d, c], mate)

    def total_copy(owner, send, recv, target):
        return pltpu.make_async_remote_copy(
            src_ref=tot.at[owner], dst_ref=tot.at[owner], send_sem=send, recv_sem=recv,
            device_id=(here, target), device_id_type=MESH,
        )

    def total_direct(d, inward=False):
        owner = (me + levs - 2 * d) % levs if inward else me
        return total_copy(owner, tot_send.at[d - 1], tot_recv.at[d - 1], (me + 2 * d) % levs)

    def total_mate(d, inward=False):
        owner = ((mate if inward else me) + levs - 2 * d) % levs
        return total_copy(owner, totm_send.at[d], totm_recv.at[d], mate)

    def column(i, total):
        rows = pl.ds(pl.multiple_of((L - 1 - i) * R, R), R)
        return total + theta_v[rows, :] * thick_v[rows, :] * LEVELS ** (-0.5)

    for c in range(chunks):
        if c == 0:
            theta_loads[0].wait()

        def relayout(i, _, c=c):
            r = c * CHUNK + i
            gath[r, slot_of(me), :] = theta_v[pl.ds(r, L, stride=R), :].astype(BF16)
            return 0

        lax.fori_loop(0, CHUNK, relayout, 0, unroll=True)
        if c == 0:
            pl.semaphore_wait(barrier, levs + 1)
        for d in range(1, half):
            direct(d, c).start()
        to_mate(0, c).start()
        if c == 0:
            for copy in theta_loads[1:] + loads[:1]:
                copy.wait()
            tot[me] = lax.fori_loop(0, L, column, jnp.zeros((R, C), F32), unroll=8)
            for d in range(1, half):
                total_direct(d).start()
            total_mate(0).start()

    for i in (1, 2):
        loads[i].wait()

    def level(i, total):
        rows = pl.ds(pl.multiple_of((L - 1 - i) * R, R), R)
        thermal = theta_v[rows, :] * thick_v[rows, :] * LEVELS ** (-0.5)
        geopot = surf_v[...] + total + 0.5 * thermal
        xh[rows, 0:C], xl[rows, 0:C] = split(geopot)
        xh[rows, C : 2 * C], xl[rows, C : 2 * C] = split(wind_v[rows, :])
        return total + thermal

    lax.fori_loop(0, L, level, jnp.zeros((R, C), F32), unroll=4)

    loads[3].wait()
    mhi_v[...], mlo_v[...] = split(op_v[...])
    per = 2
    for step in range(slots // per):
        if step == slots // per // 2:
            for d in range(1, half):
                total_direct(d, True).wait_recv()
                total_mate(d).start()
        rows = pl.ds(step * per * srows, per * srows)
        high, low = xh[rows, :], xl[rows, :]
        y = dot(high, mhi_v[...]) + dot(low, mhi_v[...]) + dot(high, mlo_v[...])
        p_s[rows, :] = y[:, 0:C]
        v_s[rows, :] = y[:, C : 2 * C]
        for j in range(per):
            g = step * per + j
            for side in range(2):
                part = y[j * srows : (j + 1) * srows, (2 + side) * C : (3 + side) * C]
                if g == 0:
                    pack[side] = part
                else:
                    pack[side] += pltpu.roll(part, g * SLOT, 1)

    def side_copy(src, dst, send, recv, side):
        return pltpu.make_async_remote_copy(
            src_ref=src.at[side], dst_ref=dst.at[side], send_sem=send.at[side], recv_sem=recv.at[side],
            device_id=((left, right)[side], me), device_id_type=MESH,
        )

    halos = [side_copy(pack, pack_in, halo_send, halo_recv, side) for side in range(2)]
    for copy in halos:
        copy.start()

    def forward(c):
        for d in range(1, half):
            direct_in(d, c).wait_recv()
            to_mate(d, c).start()

    forward(0)
    for d in range(half):
        total_mate(d, True).wait_recv()
    carry = jnp.zeros((R, C), F32)
    for owner in range(levs):
        carry = carry + jnp.where(owner > me, tot[owner], 0.0)
    ch, cl = split(carry)
    yc = dot(ch, mhi_v[0:C, :]) + dot(cl, mhi_v[0:C, :]) + dot(ch, mlo_v[0:C, :])
    cpack[0] = yc[:, 2 * C : 3 * C]
    cpack[1] = yc[:, 3 * C : 4 * C]
    chalos = [side_copy(cpack, cpack_in, chalo_send, chalo_recv, side) for side in range(2)]
    for copy in chalos:
        copy.start()

    for i in (4, 5, 6):
        loads[i].wait()

    def physics(c):
        for d in range(half):
            from_mate(d, c).wait_recv()

        def pair(i, _):
            r = c * CHUNK + 2 * i
            cols = jnp.concatenate([gath[r], gath[r + 1]], axis=1)
            res = dot(w_v[...].reshape(S * L, levs * L), cols)
            for j in range(2):
                mine = res[:, j * C : (j + 1) * C]
                scheme = jnp.broadcast_to(clos_v[pl.ds(r + j, 1), :], (L, C))
                on = jnp.broadcast_to(trig_v[pl.ds(r + j, 1), :].astype(F32), (L, C))
                chosen = mine[0:L]
                for s in range(1, S - 1):
                    chosen = jnp.where(scheme == s, mine[s * L : (s + 1) * L], chosen)
                heat[pl.ds(r + j, L, stride=R), :] = mine[(S - 1) * L :] + on * chosen
            return 0

        lax.fori_loop(0, CHUNK // 2, pair, 0, unroll=True)

    def finish():
        for copy in halos + chalos:
            copy.wait_recv()

        def edges(to_left, to_right, start, rows):
            at = lax.broadcasted_iota(jnp.int32, (rows, C), 1)
            first = pltpu.roll(to_right, (C - start) % C, 1)
            last = pltpu.roll(to_left, (2 * C - H - start) % C, 1)
            return jnp.where(at < H, first, jnp.where(at >= C - H, last, 0.0))

        common = [yc[:, f * C : (f + 1) * C] + edges(cpack_in[0], cpack_in[1], f * H, R) for f in range(2)]
        for g in range(slots):
            rows = pl.ds(g * srows, srows)
            for f, held in enumerate((p_s, v_s)):
                fix = edges(pack_in[0], pack_in[1], g * SLOT + f * H, srows)
                many = (held[rows, :] + fix).reshape(srows // R, R, C) + common[f][None]
                held[rows, :] = many.reshape(srows, C)

    for c in range(1, chunks):
        if c == chunks - 1:
            finish()
        forward(c)
        physics(c - 1)
    physics(chunks - 1)

    for c in range(chunks):
        for d in range(1, half):
            direct(d, c).wait_send()
        for d in range(half):
            to_mate(d, c).wait_send()
    for d in range(1, half):
        total_direct(d).wait_send()
    for d in range(half):
        total_mate(d).wait_send()
    for copy in halos + chalos:
        copy.wait_send()


def store_kernel(p_s, v_s, heat, p_out, v_out, h_out, hout, out_sem, hout_sem):
    L, R, C = hout.shape
    copies = [
        pltpu.make_async_copy(held, out, out_sem.at[field])
        for field, (held, out) in enumerate(((p_s, p_out), (v_s, v_out)))
    ]
    for copy in copies:
        copy.start()
    for o in range(R // PACK):
        rows = pl.ds(o * PACK, PACK)

        def one(k, _):
            hout[k, rows, :] = heat[pl.ds(pl.multiple_of(k * R + o * PACK, PACK), PACK), :].astype(BF16)
            return 0

        lax.fori_loop(0, L, one, 0, unroll=8)
        copy = pltpu.make_async_copy(hout.at[:, rows, :], h_out.at[:, rows, :], hout_sem.at[o])
        copy.start()
        copies.append(copy)
    for copy in copies:
        copy.wait()


def shards(levs, tiles, theta, thickness, wind, surface, trigger, closure, closure_weights):
    L, R, C = theta.shape
    S = closure_weights.shape[0]
    half = levs // 2
    chunks = R // CHUNK
    slots = C // SLOT
    srows = L * R // slots
    flat = (L * R, C)
    near = pl.BlockSpec(memory_space=pltpu.VMEM)
    hbm = pl.BlockSpec(memory_space=pltpu.HBM)
    vmem, dma = pltpu.VMEM, pltpu.SemaphoreType.DMA
    parts = pl.pallas_call(
        functools.partial(kernel, (levs, tiles, L, R, C, S)),
        out_shape=(
            vmem(flat, F32), vmem(flat, F32), vmem(flat, F32),
        ),
        in_specs=[hbm] * 8,
        out_specs=(near,) * 3,
        scratch_shapes=[
            vmem((L, R, C), F32), vmem(flat, F32), vmem(flat, F32),
            vmem((R, C), F32), vmem((R, C), jnp.int32), vmem((R, C), jnp.int32),
            vmem((S, L, levs * L), BF16), vmem((2 * C, 4 * C), F32), vmem((2 * C, 4 * C), BF16), vmem((2 * C, 4 * C), BF16),
            vmem((R, levs * L, C), BF16),
            vmem((L * R, 2 * C), BF16), vmem((L * R, 2 * C), BF16),
            vmem((2, srows, C), F32), vmem((2, srows, C), F32),
            vmem((levs, R, C), F32),
            vmem((2, R, C), F32), vmem((2, R, C), F32),
            dma((chunks,)), dma((7,)),
            dma((max(half - 1, 1), chunks)), dma((max(half - 1, 1), chunks)), dma((half, chunks)), dma((half, chunks)),
            dma((max(half - 1, 1),)), dma((max(half - 1, 1),)), dma((half,)), dma((half,)), dma((2,)), dma((2,)), dma((2,)), dma((2,)),
        ],
        compiler_params=pltpu.CompilerParams(
            collective_id=0, has_side_effects=True, vmem_limit_bytes=24 * 1024 * 1024
        ),
        cost_estimate=pl.CostEstimate(flops=10**9, bytes_accessed=4 * 10**6, transcendentals=0),
    )(
        *(
            pltpu.with_memory_space_constraint(value, pltpu.HBM)
            for value in (
                theta, thickness.reshape(flat), wind.reshape(flat), surface, trigger, closure,
                closure_weights, jnp.asarray(substep_operator(C)),
            )
        )
    )
    p, v, h = pl.pallas_call(
        store_kernel,
        out_shape=(
            jax.ShapeDtypeStruct(flat, F32), jax.ShapeDtypeStruct(flat, F32), jax.ShapeDtypeStruct((L, R, C), BF16)
        ),
        in_specs=[near] * 3,
        out_specs=(hbm,) * 3,
        scratch_shapes=[
            vmem((L, R, C), BF16), dma((2,)), dma((R // PACK,)),
        ],
        compiler_params=pltpu.CompilerParams(vmem_limit_bytes=16 * 1024 * 1024),
        cost_estimate=pl.CostEstimate(flops=10**6, bytes_accessed=3 * 10**6, transcendentals=0),
    )(*(pltpu.with_memory_space_constraint(part, pltpu.VMEM) for part in parts))
    return p.reshape(L, R, C), v.reshape(L, R, C), h


def solution(mesh):
    cells, sheet = P("lev", None, "tile"), P(None, "tile")
    return jax.shard_map(
        functools.partial(shards, mesh.shape["lev"], mesh.shape["tile"]),
        mesh=mesh,
        in_specs=(cells, cells, cells, sheet, sheet, sheet, P()),
        out_specs=(cells, cells, cells),
        check_vma=False,
    )
```
